32 devices in a mesh: grp: 4 (over y, core), dev: 8 (over z, x).
Axes of the slice: x: 2, y: 2, z: 4, core: 2. Of those that a mesh axis runs over, the one named last changes fastest.
Arguments:
- points: bfloat16 [12288, 128], P(('grp', 'dev')), may hold values from -6 to 6
- start_vectors: float32 [12288, 32], P(('grp', 'dev')), may hold values from -6 to 6
Outputs:
- embedding: float32 [12288, 32], P(('grp', 'dev'))
The draws below stay inside these ranges and needn't reach their ends.
All inputs are finite; a program needn't handle non-finite values.
Results may differ from the reference program's by a relative error of at most 0.005.
Values may be sent and summed in bfloat16 or wider, within the bound.
A program may use at most 128 MiB of HBM per device.

```python
import math
import jax
import jax.numpy as jnp
from jax import lax

F = 128
K = 32
ROWS_DEV = 384
ITERS = 2
NPTS = 12288


def draw_points(key, part):
    centre_total = max(2 * K, NPTS // 384)
    key_centre = jax.random.fold_in(key, 11)
    key_member = jax.random.fold_in(key, 23)
    key_noise = jax.random.fold_in(key, 37)
    key_ratio = jax.random.fold_in(key, 41)
    centres = jax.random.normal(key_centre, (centre_total, F), jnp.float32)
    noise = jax.random.normal(key_noise, (NPTS, F), jnp.float32)
    ratio = jnp.exp(jax.random.uniform(key_ratio, (NPTS, 1), jnp.float32, math.log(0.2), math.log(0.7)))
    member = jax.random.randint(key_member, (NPTS,), 0, centre_total)
    base = jnp.take(centres, member, axis=0)
    return jnp.clip(base + ratio * noise, -6.0, 6.0).astype(jnp.bfloat16)


def level_of(own_key, extent, pieces, low, largest):
    level = 1.0
    for position, blocks in pieces:
        heights = jax.random.uniform(jax.random.fold_in(jax.random.fold_in(own_key, 6), position), (blocks,), jnp.float32, low / len(pieces), largest / len(pieces))
        level = level * jnp.repeat(jnp.exp(heights), extent[position] // blocks).reshape((-1,) + (1,) * (len(extent) - 1 - position))
    return level


def bell_draw(stream_key, dims, width, reach, split=(), dtype=jnp.bfloat16):
    loudness = level_of(stream_key, dims, split, -0.22, 0.18) if split else 1.0
    result = jax.random.normal(stream_key, dims, jnp.float32) * width * loudness
    return jnp.minimum(jnp.maximum(result, -reach), reach).astype(dtype)


def setup_inputs(seed: int = 0) -> dict:
    splits = jax.random.split(jax.random.key(seed), 3)
    return {
        "points": draw_points(jax.random.fold_in(splits[2], 71), 0),
        "start_vectors": bell_draw(splits[1], (NPTS, K), 1.0, 6.0, ((0, 32),), jnp.float32),
    }


sharpness = 8.0

def unit_rows(points):
    values = points.astype(jnp.float32)
    squares = lax.optimization_barrier(jnp.sum(values * values, axis=-1, keepdims=True))
    return (values * lax.rsqrt(squares + 1e-06)).astype(jnp.bfloat16)

def reference(points, start_vectors):
    units = lax.optimization_barrier(unit_rows(points)).astype(jnp.float32)
    blocks = units.reshape(NPTS // ROWS_DEV, ROWS_DEV, F)

    def weight_rows(block):
        cosine = jnp.dot(block.astype(jnp.float32), units.T.astype(jnp.float32), precision=lax.Precision.HIGHEST, preferred_element_type=jnp.float32)
        weights = jnp.exp(sharpness * (cosine - 1.0)).astype(jnp.bfloat16)
        return lax.optimization_barrier(weights).astype(jnp.float32)
    degree = lax.map(lambda block: lax.optimization_barrier(jnp.sum(weight_rows(block), axis=1)), blocks).reshape(NPTS)
    scale = lax.rsqrt(degree)[:, None]
    vectors = start_vectors
    for sweep in range(ITERS):
        iterate = (scale * vectors).astype(jnp.bfloat16)
        iterate = lax.optimization_barrier(iterate).astype(jnp.float32)
        product = lax.map(lambda block: jnp.dot(weight_rows(block).astype(jnp.float32), iterate.astype(jnp.float32), precision=lax.Precision.HIGHEST, preferred_element_type=jnp.float32), blocks).reshape(NPTS, K)
        image = scale * product
        gram_total = jnp.dot(image.T.astype(jnp.float32), image.astype(jnp.float32), precision=lax.Precision.HIGHEST, preferred_element_type=jnp.float32)
        factor = jnp.linalg.cholesky(gram_total)
        vectors = lax.linalg.triangular_solve(factor, image.T, left_side=True, lower=True).T
    return vectors * math.sqrt(NPTS)
```

```python
import functools
import math

import jax
import jax.numpy as jnp
from jax import lax
from jax.experimental import pallas as pl
from jax.experimental.pallas import tpu as pltpu
from jax.sharding import PartitionSpec as P

MESH = pl.DeviceIdType.MESH
HIGHEST = lax.Precision.HIGHEST
SLOPE = 8.0 / math.log(2.0)
CHUNK = 128


def layout(grp, dev):
    cores = 2
    deep = 4 if dev % 4 == 0 else dev
    return grp // cores, dev // deep, deep


def kernel(Y, X, Z, pts, start, out, units, it0, it1, weights, plane_buf, line_buf,
           send, zsend, recv, gsend, grecv, lsend, lrecv):
    n = Y * X * Z
    rows = pts.shape[0]
    width = start.shape[1]
    total = 2 * n * rows
    grp = lax.axis_index("grp")
    dev = lax.axis_index("dev")
    y, c = grp // 2, grp % 2
    z, x = dev // X, dev % X

    def device(dy=0, dx=0, dz=0, dc=0):
        return (
            ((y + Y - dy) % Y) * 2 + (c + dc) % 2,
            ((z + Z - dz) % Z) * X + (x + X - dx) % X,
        )

    plane = [(a, b, d) for a in range(Y) for b in range(X) for d in range(2)][1:]

    def slot(dy, dx, dz):
        return (dy * X + dx) * Z + dz

    def view(buf, index, part):
        if part is None:
            return buf.at[index]
        half = buf.shape[1] // 2
        return buf.at[index, pl.ds(part * half, half)]

    def copy(g, buf, src, dst, part, ssem, rsem, target):
        return pltpu.make_async_remote_copy(
            src_ref=view(buf, src, part), dst_ref=view(buf, dst, part),
            send_sem=ssem, recv_sem=recv.at[g, rsem],
            device_id=target, device_id_type=MESH,
        )

    def zcopies(g, buf):
        return [
            copy(g, buf, 0, slot(0, 0, e), None, zsend.at[g, e], slot(0, 0, e), device(dz=e))
            for e in range(1, Z)
        ]

    def forwards(g, buf, dy, dx, dz):
        s = slot(dy, dx, dz)
        plan = []
        if dy == 0 and dx == 0:
            plan += [(slot(0, e, dz), None, slot(0, e, dz), device(dx=e)) for e in range(1, X)]
            plan += [(slot(e, 0, dz), None, slot(e, 0, dz), device(dy=e)) for e in range(1, Y)]
        elif dy == 0:
            plan += [(slot(e, dx, dz), 1, n + slot(e, dx, dz), device(dy=e)) for e in range(1, Y)]
        elif dx == 0:
            plan += [(slot(dy, e, dz), 0, slot(dy, e, dz), device(dx=e)) for e in range(1, X)]
        plan.append((n + s, None, 2 * n + s, device(dc=1)))
        return [
            copy(g, buf, s, dst, part, send.at[g, s, k], rsem, target)
            for k, (dst, part, rsem, target) in enumerate(plan)
        ]

    def arrived(g, buf, index, part, rsem):
        copy(g, buf, index, index, part, zsend.at[g, 0], rsem, device(dc=1)).wait_recv()

    def start_all(copies):
        for one in copies:
            one.start()

    xs = [(0, e) for e in range(1, X)]
    ys = [(e, 0) for e in range(1, Y)]
    diagonal = [(a, b) for a in range(1, Y) for b in range(1, X)]

    def launch(g, buf):
        start_all(zcopies(g, buf))
        start_all(forwards(g, buf, 0, 0, 0))

    def collect(g, buf, visit, carry, first=None, second=None):
        def sibling(dy, dx, dz, carry):
            s = slot(dy, dx, dz)
            arrived(g, buf, n + s, None, 2 * n + s)
            return visit(n + s, carry)

        def column(dz, carry):
            arrived(g, buf, slot(0, 0, dz), None, slot(0, 0, dz))
            start_all(forwards(g, buf, 0, 0, dz))
            return visit(slot(0, 0, dz), carry)

        def sides(dz, carry):
            for dy, dx in xs + ys:
                s = slot(dy, dx, dz)
                arrived(g, buf, s, None, s)
                start_all(forwards(g, buf, dy, dx, dz))
                carry = visit(s, carry)
            return sibling(0, 0, dz, carry)

        def corners(dz, carry):
            for dy, dx in diagonal:
                s = slot(dy, dx, dz)
                arrived(g, buf, s, 0, s)
                arrived(g, buf, s, 1, n + s)
                start_all(forwards(g, buf, dy, dx, dz))
                carry = visit(s, carry)
            for dy, dx in xs + ys:
                carry = sibling(dy, dx, dz, carry)
            return carry

        def rest(dz, carry):
            for dy, dx in diagonal:
                carry = sibling(dy, dx, dz, carry)
            return carry

        carry = visit(0, carry)
        carry = lax.fori_loop(1, Z, column, carry)
        if first is not None:
            first()
        carry = lax.fori_loop(0, Z, sides, carry)
        extra = second() if second is not None else None
        carry = lax.fori_loop(0, Z, corners, carry)
        carry = lax.fori_loop(0, Z, rest, carry)
        return carry, extra

    def finish(g, buf):
        for one in zcopies(g, buf):
            one.wait_send()

        def each(dz, carry):
            for dy, dx in [(0, 0)] + xs + ys + diagonal:
                for one in forwards(g, buf, dy, dx, dz):
                    one.wait_send()
            return carry

        lax.fori_loop(0, Z, each, 0)

    def plane_copies(g):
        return [
            pltpu.make_async_remote_copy(
                src_ref=plane_buf.at[g, 0], dst_ref=plane_buf.at[g, k],
                send_sem=gsend.at[g, k], recv_sem=grecv.at[g, k],
                device_id=device(dy=a, dx=b, dc=d), device_id_type=MESH,
            )
            for k, (a, b, d) in enumerate(plane, 1)
        ]

    def line_copies(g):
        return [
            pltpu.make_async_remote_copy(
                src_ref=line_buf.at[g, 0], dst_ref=line_buf.at[g, e],
                send_sem=lsend.at[g, e], recv_sem=lrecv.at[g, e],
                device_id=device(dz=e), device_id_type=MESH,
            )
            for e in range(1, Z)
        ]

    def gram_start(g, image):
        wide = jnp.concatenate([image, jnp.zeros((128 - width, rows), jnp.float32)], axis=0)
        gram = lax.dot_general(
            image, wide, (((1,), (1,)), ((), ())), precision=HIGHEST,
            preferred_element_type=jnp.float32,
        )
        packed = gram[0:8]
        for k in range(1, width // 8):
            packed = packed + pltpu.roll(gram[8 * k:8 * k + 8], width * k, 1)
        plane_buf[g, 0] = packed
        start_all(plane_copies(g))

    def gram_middle(g):
        for one in plane_copies(g):
            one.wait_recv()
        line_buf[g, 0] = jnp.sum(plane_buf[g], axis=0)
        start_all(line_copies(g))

    def gram_end(g):
        for one in line_copies(g):
            one.wait_recv()
        packed = jnp.sum(line_buf[g], axis=0)
        lane = lax.broadcasted_iota(jnp.int32, (width, 128), 1)
        row = lax.broadcasted_iota(jnp.int32, (width, 128), 0)
        parts = [
            packed if k == 1 else pltpu.roll(packed, (width - width * k) % 128, 1)
            for k in range(width // 8)
        ]
        gram = jnp.concatenate(parts, axis=0)
        table = jnp.where((lane >= width) & (lane < 2 * width), gram, 0.0)
        table = jnp.where(lane == row, 1.0, table)
        row1 = lax.broadcasted_iota(jnp.int32, (width, 1), 0)
        for j in range(width):
            column = table[:, width + j:width + j + 1]
            inverse = 1.0 / column[j:j + 1]
            factor = jnp.where(row1 > j, column * inverse, 0.0)
            table = table - factor * table[j:j + 1]
        pivots = jnp.sum(jnp.where(lane == row + width, table, 0.0), axis=1, keepdims=True)
        return (table * lax.rsqrt(pivots))[:, :width]

    partners = [device(dy=a, dx=b, dc=d) for a, b, d in plane]
    partners += [device(dz=e) for e in range(1, Z)]
    barrier = pltpu.get_barrier_semaphore()
    for partner in partners:
        pl.semaphore_signal(barrier, inc=1, device_id=partner, device_id_type=MESH)

    values = pts[...].astype(jnp.float32)
    squares = jnp.sum(values * values, axis=-1, keepdims=True)
    units[0] = (values * lax.rsqrt(squares + 1e-06)).astype(jnp.bfloat16)
    pl.semaphore_wait(barrier, len(partners))
    launch(0, units)

    def weigh(index, degree):
        own = units[0]
        for k in range(rows // CHUNK):
            piece = pl.ds(k * CHUNK, CHUNK)
            cosine = lax.dot_general(
                units[index, piece], own, (((1,), (1,)), ((), ())),
                preferred_element_type=jnp.float32,
            )
            weight = jnp.exp2(cosine * SLOPE - SLOPE).astype(jnp.bfloat16)
            weights[index, piece] = weight
            weight = weight.astype(jnp.float32)
            degree = degree + jnp.sum(weight.reshape(CHUNK // 8, 8, rows), axis=0)
        return degree

    degree, _ = collect(0, units, weigh, jnp.zeros((8, rows), jnp.float32))
    scale = lax.rsqrt(jnp.sum(degree, axis=0, keepdims=True))

    def times(buf):
        def visit(index, carry):
            return carry + jnp.dot(
                buf[index], weights[index], preferred_element_type=jnp.float32
            )
        return visit

    it0[0] = (scale * start[...].T).astype(jnp.bfloat16)
    launch(1, it0)
    product, _ = collect(1, it0, times(it0), jnp.zeros((width, rows), jnp.float32))
    image = scale * product

    iterate = scale * image
    high = iterate.astype(jnp.bfloat16)
    it1[0, :width] = high
    it1[0, width:] = (iterate - high.astype(jnp.float32)).astype(jnp.bfloat16)
    launch(2, it1)
    gram_start(0, image)
    product, inverse = collect(
        2, it1, times(it1), jnp.zeros((2 * width, rows), jnp.float32),
        first=lambda: gram_middle(0), second=lambda: gram_end(0),
    )
    product = scale * (product[:width] + product[width:])
    image = jnp.dot(inverse, product, precision=HIGHEST, preferred_element_type=jnp.float32)

    gram_start(1, image)
    gram_middle(1)
    inverse = gram_end(1)
    vectors = jnp.dot(inverse, image, precision=HIGHEST, preferred_element_type=jnp.float32)
    out[...] = (vectors * math.sqrt(total)).T

    for g, buf in enumerate((units, it0, it1)):
        finish(g, buf)
    for g in range(2):
        for one in plane_copies(g) + line_copies(g):
            one.wait_send()


def body(points, start_vectors):
    rows, features = points.shape
    width = start_vectors.shape[1]
    Y, X, Z = layout(lax.axis_size("grp"), lax.axis_size("dev"))
    n = Y * X * Z
    slots = 2 * n
    shapes = [
        pltpu.VMEM((slots, rows, features), jnp.bfloat16),
        pltpu.VMEM((slots, width, rows), jnp.bfloat16),
        pltpu.VMEM((slots, 2 * width, rows), jnp.bfloat16),
        pltpu.VMEM((slots, rows, rows), jnp.bfloat16),
        pltpu.VMEM((2, 2 * X * Y, 8, 128), jnp.float32),
        pltpu.VMEM((2, Z, 8, 128), jnp.float32),
        pltpu.SemaphoreType.DMA((3, n, X + Y - 1)),
        pltpu.SemaphoreType.DMA((3, Z)),
        pltpu.SemaphoreType.DMA((3, 3 * n)),
        pltpu.SemaphoreType.DMA((2, 2 * X * Y)),
        pltpu.SemaphoreType.DMA((2, 2 * X * Y)),
        pltpu.SemaphoreType.DMA((2, Z)),
        pltpu.SemaphoreType.DMA((2, Z)),
    ]
    held = slots * rows * 2 * (features + 3 * width + rows)
    return pl.pallas_call(
        functools.partial(kernel, Y, X, Z),
        out_shape=jax.ShapeDtypeStruct((rows, width), jnp.float32),
        in_specs=[pl.BlockSpec(memory_space=pltpu.VMEM)] * 2,
        out_specs=pl.BlockSpec(memory_space=pltpu.VMEM),
        scratch_shapes=shapes,
        compiler_params=pltpu.CompilerParams(
            collective_id=0, has_side_effects=True, vmem_limit_bytes=held + (5 << 20)
        ),
    )(points, start_vectors)


def solution(mesh):
    placed = (P(("grp", "dev"), None), P(("grp", "dev"), None))
    return jax.shard_map(
        body, mesh=mesh, in_specs=placed, out_specs=P(("grp", "dev"), None), check_vma=False
    )
```

```python
import functools
import math

import jax
import jax.numpy as jnp
from jax import lax
from jax.experimental import pallas as pl
from jax.experimental.pallas import tpu as pltpu
from jax.sharding import PartitionSpec as P

MESH = pl.DeviceIdType.MESH
HIGHEST = lax.Precision.HIGHEST
SLOPE = 8.0 / math.log(2.0)
CHUNK = 128


def layout(grp, dev):
    cores = 2
    deep = 4 if dev % 4 == 0 else dev
    return grp // cores, dev // deep, deep


def kernel(Y, X, Z, pts, start, out, units, line, it0, it1, weights, degrees, deg_out, deg_in,
           part_out, part_in, plane_buf, line_buf, usend, urecv, fsend, zsend, zrecv,
           dsend, drecv, psend, precv, gsend, grecv, lsend, lrecv):
    chips = Y * X
    panels = 2 * chips
    rows = pts.shape[0]
    width = start.shape[1]
    total = panels * Z * rows
    grp = lax.axis_index("grp")
    dev = lax.axis_index("dev")
    y, c = grp // 2, grp % 2
    z, x = dev // X, dev % X

    def ahead(k):
        a, b, d = (k // X) % Y, k % X, k // chips
        return ((y + a) % Y) * 2 + (c + d) % 2, z * X + (x + b) % X

    def behind(k):
        a, b, d = (k // X) % Y, k % X, k // chips
        return ((y + Y - a) % Y) * 2 + (c + d) % 2, z * X + (x + X - b) % X

    def below(e):
        return grp, ((z + Z - e) % Z) * X + x

    def remote(src, dst, ssem, rsem, target):
        return pltpu.make_async_remote_copy(
            src_ref=src, dst_ref=dst, send_sem=ssem, recv_sem=rsem,
            device_id=target, device_id_type=MESH,
        )

    def unit_copy(k):
        return remote(units.at[0], units.at[k], usend.at[k], urecv.at[k], behind(k))

    def unit_forward(k):
        return remote(
            units.at[k], units.at[chips + k], fsend.at[k], urecv.at[chips + k], behind(chips)
        )

    def line_copy(g, buf, e):
        return remote(buf.at[0], buf.at[e], zsend.at[g, e], zrecv.at[g, e], below(e))

    def degree_copy(k):
        return remote(deg_out.at[k], deg_in.at[k], dsend.at[k], drecv.at[k], ahead(k))

    def part_copy(g, k):
        return remote(
            part_out.at[g, k], part_in.at[g, k], psend.at[g, k], precv.at[g, k], ahead(k)
        )

    def plane_copy(g, k):
        return remote(
            plane_buf.at[g, 0], plane_buf.at[g, k], gsend.at[g, k], grecv.at[g, k], behind(k)
        )

    def plane_copies(g):
        return [plane_copy(g, k) for k in range(1, panels)]

    def line_copies(g):
        return [
            remote(line_buf.at[g, 0], line_buf.at[g, e], lsend.at[g, e], lrecv.at[g, e], below(e))
            for e in range(1, Z)
        ]

    def start_all(copies):
        for one in copies:
            one.start()

    def over(low, high, act):
        def step(k, carry):
            act(k)
            return carry
        lax.fori_loop(low, high, step, 0)

    def gram_start(g, image):
        wide = jnp.concatenate([image, jnp.zeros((128 - width, rows), jnp.float32)], axis=0)
        gram = lax.dot_general(
            image, wide, (((1,), (1,)), ((), ())), precision=HIGHEST,
            preferred_element_type=jnp.float32,
        )
        packed = gram[0:8]
        for k in range(1, width // 8):
            packed = packed + pltpu.roll(gram[8 * k:8 * k + 8], width * k, 1)
        plane_buf[g, 0] = packed
        start_all(plane_copies(g))

    def gram_middle(g):
        for one in plane_copies(g):
            one.wait_recv()
        line_buf[g, 0] = jnp.sum(plane_buf[g], axis=0)
        start_all(line_copies(g))

    def gram_end(g):
        for one in line_copies(g):
            one.wait_recv()
        packed = jnp.sum(line_buf[g], axis=0)
        lane = lax.broadcasted_iota(jnp.int32, (width, 128), 1)
        row = lax.broadcasted_iota(jnp.int32, (width, 128), 0)
        parts = [
            packed if k == 1 else pltpu.roll(packed, (width - width * k) % 128, 1)
            for k in range(width // 8)
        ]
        gram = jnp.concatenate(parts, axis=0)
        table = jnp.where((lane >= width) & (lane < 2 * width), gram, 0.0)
        table = jnp.where(lane == row, 1.0, table)
        row1 = lax.broadcasted_iota(jnp.int32, (width, 1), 0)
        for j in range(width):
            column = table[:, width + j:width + j + 1]
            inverse = 1.0 / column[j:j + 1]
            factor = jnp.where(row1 > j, column * inverse, 0.0)
            table = table - factor * table[j:j + 1]
        pivots = jnp.sum(jnp.where(lane == row + width, table, 0.0), axis=1, keepdims=True)
        return (table * lax.rsqrt(pivots))[:, :width]

    partners = [behind(k) for k in range(1, panels)] + [below(e) for e in range(1, Z)]
    barrier = pltpu.get_barrier_semaphore()
    for partner in partners:
        pl.semaphore_signal(barrier, inc=1, device_id=partner, device_id_type=MESH)

    values = pts[...].astype(jnp.float32)
    squares = jnp.sum(values * values, axis=-1, keepdims=True)
    own_units = (values * lax.rsqrt(squares + 1e-06)).astype(jnp.bfloat16)
    units[0] = own_units
    line[0] = own_units
    pl.semaphore_wait(barrier, len(partners))
    start_all([line_copy(0, line, e) for e in range(1, Z)])
    start_all([unit_copy(k) for k in range(1, chips + 1)])

    def weigh(k, e):
        theirs = units[k]
        degree = degrees[k]
        for piece in range(rows // CHUNK):
            piece = pl.ds(piece * CHUNK, CHUNK)
            cosine = lax.dot_general(
                line[e, piece], theirs, (((1,), (1,)), ((), ())),
                preferred_element_type=jnp.float32,
            )
            weight = jnp.exp2(cosine * SLOPE - SLOPE).astype(jnp.bfloat16)
            weights[k, e, piece] = weight
            weight = weight.astype(jnp.float32)
            degree = degree + jnp.sum(weight.reshape(CHUNK // 8, 8, rows), axis=0)
        degrees[k] = degree

    def near(k):
        @pl.when(k > 0)
        def _():
            unit_copy(k).wait_recv()

        @pl.when((k > 0) & (k < chips))
        def _():
            unit_forward(k).start()

        weigh(k, 0)

    def far(e):
        line_copy(0, line, e).wait_recv()
        over(0, panels, lambda k: weigh(k, e))

    def last(step):
        k = (step + 1) % panels
        weigh(k, Z - 1)
        deg_out[k] = jnp.sum(degrees[k], axis=0, keepdims=True)

        @pl.when(k > 0)
        def _():
            degree_copy(k).start()

    degrees[...] = jnp.zeros_like(degrees)
    over(0, panels, near)
    over(1, Z - 1, far)
    line_copy(0, line, Z - 1).wait_recv()
    over(0, panels, last)
    turned = start[...].T
    deg_in[0] = deg_out[0]
    over(1, panels, lambda k: degree_copy(k).wait_recv())
    scale = lax.rsqrt(jnp.sum(deg_in[...], axis=0))

    def product_of(g, buf, k):
        part = jnp.dot(buf[0], weights[k, 0], preferred_element_type=jnp.float32)
        for e in range(1, Z):
            part = part + jnp.dot(buf[e], weights[k, e], preferred_element_type=jnp.float32)
        if part.shape[0] > width:
            part = part[:width] + part[width:]
        return part

    def spread(g, buf):
        for e in range(1, Z):
            line_copy(g + 1, buf, e).wait_recv()

        def send(k):
            part_out[g, k] = product_of(g, buf, k)
            part_copy(g, k).start()

        over(1, panels, send)
        part_in[g, 0] = product_of(g, buf, 0)

    def collect(g):
        over(1, panels, lambda k: part_copy(g, k).wait_recv())
        return jnp.sum(part_in[g], axis=0)

    it0[0] = (scale * turned).astype(jnp.bfloat16)
    start_all([line_copy(1, it0, e) for e in range(1, Z)])
    spread(0, it0)
    image = scale * collect(0)

    iterate = scale * image
    high = iterate.astype(jnp.bfloat16)
    it1[0, :width] = high
    it1[0, width:] = (iterate - high.astype(jnp.float32)).astype(jnp.bfloat16)
    start_all([line_copy(2, it1, e) for e in range(1, Z)])
    gram_start(0, image)
    gram_middle(0)
    spread(1, it1)
    inverse = gram_end(0)
    product = scale * collect(1)
    image = jnp.dot(inverse, product, precision=HIGHEST, preferred_element_type=jnp.float32)

    gram_start(1, image)
    gram_middle(1)
    inverse = gram_end(1)
    vectors = jnp.dot(inverse, image, precision=HIGHEST, preferred_element_type=jnp.float32)
    out[...] = (vectors * math.sqrt(total)).T

    over(1, chips + 1, lambda k: unit_copy(k).wait_send())
    over(1, chips, lambda k: unit_forward(k).wait_send())
    over(1, panels, lambda k: degree_copy(k).wait_send())
    for g, buf in enumerate((line, it0, it1)):
        for e in range(1, Z):
            line_copy(g, buf, e).wait_send()
    for g in range(2):
        over(1, panels, lambda k: part_copy(g, k).wait_send())
        for one in plane_copies(g) + line_copies(g):
            one.wait_send()


def body(points, start_vectors):
    rows, features = points.shape
    width = start_vectors.shape[1]
    Y, X, Z = layout(lax.axis_size("grp"), lax.axis_size("dev"))
    panels = 2 * Y * X
    dma = pltpu.SemaphoreType.DMA
    shapes = [
        pltpu.VMEM((panels, rows, features), jnp.bfloat16),
        pltpu.VMEM((Z, rows, features), jnp.bfloat16),
        pltpu.VMEM((Z, width, rows), jnp.bfloat16),
        pltpu.VMEM((Z, 2 * width, rows), jnp.bfloat16),
        pltpu.VMEM((panels, Z, rows, rows), jnp.bfloat16),
        pltpu.VMEM((panels, 8, rows), jnp.float32),
        pltpu.VMEM((panels, 1, rows), jnp.float32),
        pltpu.VMEM((panels, 1, rows), jnp.float32),
        pltpu.VMEM((2, panels, width, rows), jnp.float32),
        pltpu.VMEM((2, panels, width, rows), jnp.float32),
        pltpu.VMEM((2, panels, 8, 128), jnp.float32),
        pltpu.VMEM((2, Z, 8, 128), jnp.float32),
        dma((panels,)), dma((panels,)), dma((panels,)),
        dma((3, Z)), dma((3, Z)),
        dma((panels,)), dma((panels,)),
        dma((2, panels)), dma((2, panels)),
        dma((2, panels)), dma((2, panels)),
        dma((2, Z)), dma((2, Z)),
    ]
    held = 2 * panels * rows * (features + Z * rows + 8 * width) + 2 * Z * rows * (features + 3 * width)
    return pl.pallas_call(
        functools.partial(kernel, Y, X, Z),
        out_shape=jax.ShapeDtypeStruct((rows, width), jnp.float32),
        in_specs=[pl.BlockSpec(memory_space=pltpu.VMEM)] * 2,
        out_specs=pl.BlockSpec(memory_space=pltpu.VMEM),
        scratch_shapes=shapes,
        compiler_params=pltpu.CompilerParams(
            collective_id=0, has_side_effects=True, vmem_limit_bytes=held + (5 << 20)
        ),
    )(points, start_vectors)


def solution(mesh):
    placed = (P(("grp", "dev"), None), P(("grp", "dev"), None))
    return jax.shard_map(
        body, mesh=mesh, in_specs=placed, out_specs=P(("grp", "dev"), None), check_vma=False
    )
```
